32 devices in a mesh: grp: 2 (over y), gx: 4 (over z), gy: 4 (over x, core).
Axes of the slice: x: 2, y: 2, z: 4, core: 2. Of those that a mesh axis runs over, the one named last changes fastest.
Arguments:
- counts: int32 [256, 256, 256], P(('grp', 'gx'), 'gy'), parts along dimension 0, may hold values from -40 to 999
Outputs:
- denoised: float32 [256, 256, 256], P(('grp', 'gx'), 'gy'), parts along dimension 0
The draws below stay inside these ranges and needn't reach their ends.
There are 2 independent parts, one for each index of `grp`. The reference program is written for one: setup_inputs(seed, part) draws one part's arguments, and reference() takes and returns one part's arrays. A program takes and returns all parts, laid end to end along the dimension named above; each array names one. Nothing has to cross between parts.
All inputs are finite; a program needn't handle non-finite values.
Results may differ from the reference program's by a relative error of at most 0.00005.
Values sent between devices are 32-bit elements; how exact they have to be, the bound alone decides.
A program may use at most 64 MiB of HBM per device.

```python
import math
import jax
import jax.numpy as jnp
from jax import lax

NT = 256
LEVELS = 3
ITERS = 2
NX = 128
NY = 256


def plant(entries, own_key, low, top_value):
    place = [jax.random.randint(jax.random.fold_in(own_key, axis), (), 0, length) for axis, length in enumerate(entries.shape)]
    longest = entries.shape.index(max(entries.shape))
    beside = place[:longest] + [(place[longest] + 1) % entries.shape[longest]] + place[longest + 1:]
    return entries.at[tuple(place)].set(low).at[tuple(beside)].set(top_value)


def setup_inputs(seed: int = 0, part: int = 0) -> dict:
    keys = jax.random.split(jax.random.key(seed), 2)
    own_keys = jax.random.split(jax.random.fold_in(keys[1], part), 2)
    counts = plant(jax.random.randint(own_keys[0], (NX, NY, NT), -40, 1000), jax.random.fold_in(own_keys[0], 1), -40, 999).astype(jnp.int32)
    return {"counts": counts}


ROOT_THREE = math.sqrt(3.0)
TAP_SCALE = 4.0 * math.sqrt(2.0)
LOW_TAPS = [(1.0 + ROOT_THREE) / TAP_SCALE, (3.0 + ROOT_THREE) / TAP_SCALE, (3.0 - ROOT_THREE) / TAP_SCALE, (1.0 - ROOT_THREE) / TAP_SCALE]
HIGH_TAPS = [LOW_TAPS[3], -LOW_TAPS[2], LOW_TAPS[1], -LOW_TAPS[0]]
STEP_SIZE = 1.0
THRESHOLD = 0.1

def analyse(values, axis_dim):
    length = values.shape[axis_dim]
    low_part = None
    high_part = None
    for tap_index in range(4):
        rolled = jnp.roll(values, -tap_index, axis=axis_dim)
        picked = lax.slice_in_dim(rolled, 0, length, 2, axis_dim)
        if low_part is None:
            low_part = LOW_TAPS[tap_index] * picked
            high_part = HIGH_TAPS[tap_index] * picked
        else:
            low_part = low_part + LOW_TAPS[tap_index] * picked
            high_part = high_part + HIGH_TAPS[tap_index] * picked
    return (low_part, high_part)

def synthesise(low_part, high_part, axis_dim):
    summed = None
    for tap_index in range(4):
        weighted = LOW_TAPS[tap_index] * low_part + HIGH_TAPS[tap_index] * high_part
        spread = jnp.stack([weighted, jnp.zeros_like(weighted)], axis=axis_dim + 1)
        new_shape = list(weighted.shape)
        new_shape[axis_dim] = new_shape[axis_dim] * 2
        spread = spread.reshape(new_shape)
        rolled = jnp.roll(spread, tap_index, axis=axis_dim)
        summed = rolled if summed is None else summed + rolled
    return summed

def forward_all(volume):
    details = []
    approx = volume
    for level_no in range(LEVELS):
        subbands = []
        for x_band in analyse(approx, 0):
            for y_band in analyse(x_band, 1):
                t_low, t_high = analyse(y_band, 2)
                subbands.append(t_low)
                subbands.append(t_high)
        approx = subbands[0]
        details.append(subbands[1:])
    return (details, approx)

def inverse_all(details, approx):
    current = approx
    for level_no in reversed(range(LEVELS)):
        subbands = [current] + list(details[level_no])
        x_parts = []
        for x_pick in range(2):
            y_parts = []
            for y_pick in range(2):
                first = subbands[4 * x_pick + 2 * y_pick]
                second = subbands[4 * x_pick + 2 * y_pick + 1]
                y_parts.append(synthesise(first, second, 2))
            x_parts.append(synthesise(y_parts[0], y_parts[1], 1))
        current = synthesise(x_parts[0], x_parts[1], 0)
    return current

def shrink(values):
    return values - jnp.clip(values, -THRESHOLD, THRESHOLD)

def reference(counts):
    scaled = counts.astype(jnp.float32)
    observed = scaled * (1.0 / 64.0)
    weight = 1.0 / (1.0 + jnp.abs(scaled) * (1.0 / 64.0))
    grad_details, grad_approx = forward_all(-(weight * observed))
    details = [[shrink(-STEP_SIZE * entry) for entry in level_bands] for level_bands in grad_details]
    approx = -STEP_SIZE * grad_approx
    for turn_no in range(ITERS - 1):
        rebuilt = inverse_all(details, approx)
        grad_details, grad_approx = forward_all(weight * (rebuilt - observed))
        details = [[shrink(old_entry - STEP_SIZE * new_entry) for old_entry, new_entry in zip(old_bands, new_bands)] for old_bands, new_bands in zip(details, grad_details)]
        approx = approx - STEP_SIZE * grad_approx
    return inverse_all(details, approx)
```

```python
import functools
import math

import jax
import jax.numpy as jnp
import ml_dtypes
import numpy as np
from jax import lax
from jax.experimental import pallas as pl
from jax.experimental.pallas import tpu as pltpu
from jax.sharding import PartitionSpec as P

ROOT_THREE = math.sqrt(3.0)
TAP_SCALE = 4.0 * math.sqrt(2.0)
H = [
    (1.0 + ROOT_THREE) / TAP_SCALE,
    (3.0 + ROOT_THREE) / TAP_SCALE,
    (3.0 - ROOT_THREE) / TAP_SCALE,
    (1.0 - ROOT_THREE) / TAP_SCALE,
]
G = [H[3], -H[2], H[1], -H[0]]
THRESHOLD = 0.1
MESH = pl.DeviceIdType.MESH
F32 = jnp.float32
BF16 = jnp.bfloat16


def split_matrix(matrix):
    high = matrix.astype(ml_dtypes.bfloat16)
    low = (matrix - high.astype(np.float32)).astype(ml_dtypes.bfloat16)
    return np.stack([high, low])


def time_matrices(length, padded):
    matrix = np.zeros((padded, padded), np.float32)
    for k in range(length // 2):
        for j in range(4):
            matrix[(2 * k + j) % length, k] += H[j]
            matrix[(2 * k + j) % length, length // 2 + k] += G[j]
    return split_matrix(matrix), split_matrix(np.ascontiguousarray(matrix.T))


def times(values, matrix_ref):
    high = values.astype(BF16)
    low = (values - high.astype(F32)).astype(BF16)
    first = matrix_ref[0]
    second = matrix_ref[1]
    dot = functools.partial(jnp.dot, preferred_element_type=F32)
    return dot(high, first) + (dot(low, first) + dot(high, second))


def shrink(values):
    return values - jnp.clip(values, -THRESHOLD, THRESHOLD)


def low_of(e):
    return (H[0] * e[0] + H[1] * e[1]) + (H[2] * e[2] + H[3] * e[3])


def high_of(e):
    return (G[0] * e[0] + G[1] * e[1]) + (G[2] * e[2] + G[3] * e[3])


def even_of(lo, hi, lo_before, hi_before):
    return (H[0] * lo + G[0] * hi) + (H[2] * lo_before + G[2] * hi_before)


def odd_of(lo, hi, lo_before, hi_before):
    return (H[1] * lo + G[1] * hi) + (H[3] * lo_before + G[3] * hi_before)


def loop(count, body, unroll=1):
    def step(i, carry):
        body(i)
        return carry

    lax.fori_loop(0, count, step, 0, unroll=unroll)


def rows(start, size):
    return pl.ds(pl.multiple_of(start, 8), size)


def kernel(
    nx, ny,
    counts, m1, m1t, m2, m2t, m3, m3t, out,
    t0, a0, c1, e1, t2, a2, c2, e2, t3, a3, c3,
    s3, p3, d2, s2, p2, d1, s1, p1, reb, edge,
    f0x, f0y, f0c, f0xr, f0yr, f0cr,
    f1x, f1y, f1c, f1xr, f1yr, f1cr,
    i1x, i1y, i1c, i1xr, i1yr, i1cr,
    i2x, i2y, i2c, i2xr, i2yr, i2cr,
    send_sem, recv_sem,
):
    gx = lax.axis_index("gx")
    gy = lax.axis_index("gy")
    x_after, x_before = lax.rem(gx + 1, nx), lax.rem(gx + nx - 1, nx)
    y_after, y_before = lax.rem(gy + 1, ny), lax.rem(gy + ny - 1, ny)
    before = [{"gx": x_before}, {"gy": y_before}, {"gx": x_before, "gy": y_before}]
    after = [{"gx": x_after}, {"gy": y_after}, {"gx": x_after, "gy": y_after}]

    barrier = pltpu.get_barrier_semaphore()
    for other in before + after:
        pl.semaphore_signal(barrier, inc=1, device_id=other, device_id_type=MESH)

    def send(round_no, sources, targets, others):
        copies = []
        for n in range(3):
            copy = pltpu.make_async_remote_copy(
                src_ref=sources[n],
                dst_ref=targets[n],
                send_sem=send_sem.at[3 * round_no + n],
                recv_sem=recv_sem.at[3 * round_no + n],
                device_id=others[n],
                device_id_type=MESH,
            )
            copy.start()
            copies.append(copy)
        return copies

    def wait(copies):
        for copy in copies:
            copy.wait()

    def residual(count, rebuilt):
        observed = count.astype(F32) * (1.0 / 64.0)
        weight = 1.0 / (1.0 + jnp.abs(observed))
        if rebuilt is None:
            return weight * observed
        return weight * (observed - rebuilt)

    def iteration(number):
        first = number == 0

        def old(ref, *index):
            return 0.0 if first else ref[index]

        for i in range(2):
            for th in range(2):
                f0x[th, i * 64 : (i + 1) * 64, :] = residual(
                    counts[i, :, th * 128 : (th + 1) * 128],
                    None if first else reb[th, i * 64 : (i + 1) * 64, :],
                )

        def edge_row(x):
            for th in range(2):
                edge[th, rows(x * 8, 8), :] = residual(
                    counts[x, 0:8, th * 128 : (th + 1) * 128],
                    None if first else reb[th, rows(x * 64, 8), :],
                )

        loop(32, edge_row, unroll=4)
        for th in range(2):
            for j in range(2):
                f0y[th, j * 32 : (j + 1) * 32, :] = edge[th, pl.ds(j, 32, stride=8), :]
            for i in range(2):
                f0c[th, i * 8 : (i + 1) * 8, :] = f0x[th, i * 64 : i * 64 + 8, :]
        if first:
            pl.semaphore_wait(barrier, 6)
        f0 = send(4 * number, [f0x, f0y, f0c], [f0xr, f0yr, f0cr], before)

        def time_rows(n):
            count = counts[pl.ds(n * 4, 4)].reshape(256, 256)
            if first:
                values = residual(count, None)
            else:
                rebuilt = jnp.concatenate(
                    [reb[0, rows(n * 256, 256), :], reb[1, rows(n * 256, 256), :]], axis=1
                )
                values = residual(count, rebuilt)
            result = times(values, m1)
            for i in range(4):
                for tb in range(2):
                    t0[tb, rows((n * 4 + i) * 72, 64), :] = result[
                        i * 64 : (i + 1) * 64, tb * 128 : (tb + 1) * 128
                    ]

        loop(8, time_rows)
        wait(f0)
        result = times(jnp.concatenate([f0xr[0], f0xr[1]], axis=1), m1)
        for i in range(2):
            for tb in range(2):
                t0[tb, (32 + i) * 72 : (32 + i) * 72 + 64, :] = result[
                    i * 64 : (i + 1) * 64, tb * 128 : (tb + 1) * 128
                ]
        result = times(jnp.concatenate([f0yr[0], f0yr[1]], axis=1), m1)
        for j in range(2):
            for tb in range(2):
                t0[tb, pl.ds(64 + j, 32, stride=72), :] = result[
                    j * 32 : (j + 1) * 32, tb * 128 : (tb + 1) * 128
                ]
        result = times(jnp.concatenate([f0cr[0], f0cr[1]], axis=1), m1)
        for i in range(2):
            for tb in range(2):
                t0[tb, (32 + i) * 72 + 64 : (33 + i) * 72, :] = result[
                    i * 8 : (i + 1) * 8, tb * 128 : (tb + 1) * 128
                ]

        def x_level1(k):
            for tb in range(2):
                e = [t0[tb, rows((2 * k + j) * 72, 72), :] for j in range(4)]
                a0[tb, rows(k * 72, 72), :] = low_of(e)
                a0[2 + tb, rows(k * 72, 72), :] = high_of(e)

        loop(16, x_level1)

        def y_level1(k):
            for xb in range(2):
                for tb in range(2):
                    e = [a0[2 * xb + tb, pl.ds(k * 72 + j, 32, stride=2), :] for j in range(4)]
                    for yb in range(2):
                        value = high_of(e) if yb else low_of(e)
                        band = 4 * xb + 2 * yb + tb
                        if band == 0:
                            e1[rows(k * 40, 32), :] = value
                        else:
                            place = rows((k + 1) * 40 + 8, 32)
                            c1[band - 1, place, :] = shrink(old(c1, band - 1, place, slice(None)) + value)

        loop(16, y_level1)

        for i in range(6):
            f1x[i * 32 : (i + 1) * 32, :] = e1[i * 40 : i * 40 + 32, :]
            f1c[i * 8 : (i + 1) * 8, :] = e1[i * 40 : i * 40 + 8, :]
            f1y[i * 16 : (i + 1) * 16, :] = e1[pl.ds(i, 16, stride=40), :]
        f1 = send(4 * number + 1, [f1x, f1y, f1c], [f1xr, f1yr, f1cr], before)
        for b in range(7):
            i1x[b * 32 : (b + 1) * 32, :] = c1[b, 16 * 40 + 8 : 17 * 40, :]
            i1y[b * 16 : (b + 1) * 16, :] = c1[b, pl.ds(40 + 39, 16, stride=40), :]
            i1c[b * 8 : (b + 1) * 8, :] = c1[b, 16 * 40 + 32 : 17 * 40, :]
        i1 = send(4 * number + 2, [i1x, i1y, i1c], [i1xr, i1yr, i1cr], after)
        wait(f1)
        for i in range(6):
            e1[(16 + i) * 40 : (16 + i) * 40 + 32, :] = f1xr[i * 32 : (i + 1) * 32, :]
            e1[(16 + i) * 40 + 32 : (17 + i) * 40, :] = f1cr[i * 8 : (i + 1) * 8, :]
            e1[pl.ds(32 + i, 16, stride=40), :] = f1yr[i * 16 : (i + 1) * 16, :]

        def time_level2(n):
            t2[rows(n * 176, 176), :] = times(e1[rows(n * 176, 176), :], m2)

        loop(5, time_level2)

        def x_level2(k):
            e = [t2[rows((2 * k + j) * 40, 40), :] for j in range(4)]
            a2[0, rows(k * 40, 40), :] = low_of(e)
            a2[1, rows(k * 40, 40), :] = high_of(e)

        loop(10, x_level2)

        def y_level2_low(k):
            e = [a2[0, pl.ds(k * 40 + j, 18, stride=2), :] for j in range(4)]
            e2[rows(k * 24, 18), :] = low_of(e)

        loop(10, y_level2_low)

        def y_level2(k):
            place = rows((k + 2) * 24 + 8, 16)
            for xb in range(2):
                e = [a2[xb, pl.ds(k * 40 + j, 16, stride=2), :] for j in range(4)]
                for yb in range(2):
                    value = high_of(e) if yb else low_of(e)
                    b = 2 * xb + yb
                    c2[b, place, :] = shrink(old(c2, b, place, slice(None)) + value)

        loop(8, y_level2)

        t3[...] = times(e2[...], m3)

        def x_level3(k):
            e = [t3[rows((2 * k + j) * 24, 24), :] for j in range(4)]
            a3[0, rows(k * 24, 24), :] = low_of(e)
            a3[1, rows(k * 24, 24), :] = high_of(e)

        loop(4, x_level3)

        lane = lax.broadcasted_iota(jnp.int32, (8, 128), 1)

        def y_level3(k):
            place = rows((k + 2) * 16 + 8, 8)
            for xb in range(2):
                e = [a3[xb, pl.ds(k * 24 + j, 8, stride=2), :] for j in range(4)]
                for yb in range(2):
                    value = high_of(e) if yb else low_of(e)
                    b = 2 * xb + yb
                    value = old(c3, b, place, slice(None)) + value
                    if b == 0:
                        c3[b, place, :] = jnp.where(lane < 32, value, shrink(value))
                    else:
                        c3[b, place, :] = shrink(value)

        loop(4, y_level3)

        for b in range(4):
            for i in range(2):
                n = 2 * b + i
                i2x[n * 16 : (n + 1) * 16, :] = c2[b, (8 + i) * 24 + 8 : (9 + i) * 24, :]
                i2x[128 + n * 8 : 128 + (n + 1) * 8, :] = c3[b, (4 + i) * 16 + 8 : (5 + i) * 16, :]
                i2y[n * 8 : (n + 1) * 8, :] = c2[b, pl.ds(2 * 24 + 22 + i, 8, stride=24), :]
                i2y[64 + n * 4 : 64 + (n + 1) * 4, :] = c3[b, pl.ds(2 * 16 + 14 + i, 4, stride=16), :]
                i2c[n * 8 : (n + 1) * 8, :] = c2[b, (8 + i) * 24 + 16 : (9 + i) * 24, :]
                i2c[64 + n * 8 : 64 + (n + 1) * 8, :] = c3[b, (4 + i) * 16 + 8 : (5 + i) * 16, :]
        i2 = send(4 * number + 3, [i2x, i2y, i2c], [i2xr, i2yr, i2cr], after)
        wait(i2)
        for b in range(4):
            for i in range(2):
                n = 2 * b + i
                c2[b, i * 24 + 8 : (i + 1) * 24, :] = i2xr[n * 16 : (n + 1) * 16, :]
                c3[b, i * 16 + 8 : (i + 1) * 16, :] = i2xr[128 + n * 8 : 128 + (n + 1) * 8, :]
                c2[b, pl.ds(2 * 24 + 6 + i, 8, stride=24), :] = i2yr[n * 8 : (n + 1) * 8, :]
                c3[b, pl.ds(2 * 16 + 6 + i, 4, stride=16), :] = i2yr[64 + n * 4 : 64 + (n + 1) * 4, :]
                c2[b, i * 24 : i * 24 + 8, :] = i2cr[n * 8 : (n + 1) * 8, :]
                c3[b, i * 16 : i * 16 + 8, :] = i2cr[64 + n * 8 : 64 + (n + 1) * 8, :]

        for b in range(4):
            s3[b] = times(c3[b], m3t)

        def x_up3(k):
            for yb in range(2):
                e = [s3[b, rows((k + d) * 16, 16), :] for d in (1, 0) for b in (yb, 2 + yb)]
                p3[yb, rows(2 * k * 16, 16), :] = even_of(*e)
                p3[yb, rows((2 * k + 1) * 16, 16), :] = odd_of(*e)

        loop(5, x_up3)

        def y_up3(r):
            e = [p3[b, pl.ds(r * 16 + d, 9), :] for d in (7, 6) for b in (0, 1)]
            d2[pl.ds(r * 24 + 6, 9, stride=2), :] = even_of(*e)
            d2[pl.ds(r * 24 + 7, 9, stride=2), :] = odd_of(*e)

        loop(10, y_up3)

        lanes = lax.broadcasted_iota(jnp.int32, (240, 128), 1)
        s2[0] = times(jnp.where(lanes < 64, d2[...], c2[0]), m2t)
        for b in range(1, 4):
            s2[b] = times(c2[b], m2t)

        def x_up2(k):
            for yb in range(2):
                e = [s2[b, rows((k + d) * 24, 24), :] for d in (1, 0) for b in (yb, 2 + yb)]
                p2[yb, rows(2 * k * 24, 24), :] = even_of(*e)
                p2[yb, rows((2 * k + 1) * 24, 24), :] = odd_of(*e)

        loop(9, x_up2)

        def y_up2(r):
            e = [p2[b, pl.ds(r * 24 + d, 17), :] for d in (7, 6) for b in (0, 1)]
            d1[pl.ds(r * 40 + 6, 17, stride=2), :] = even_of(*e)
            d1[pl.ds(r * 40 + 7, 17, stride=2), :] = odd_of(*e)

        loop(18, y_up2)

        wait(i1)
        for b in range(7):
            c1[b, 8:40, :] = i1xr[b * 32 : (b + 1) * 32, :]
            c1[b, pl.ds(40 + 7, 16, stride=40), :] = i1yr[b * 16 : (b + 1) * 16, :]
            c1[b, 0:8, :] = i1cr[b * 8 : (b + 1) * 8, :]

        def time_up1(n):
            place = rows(n * 136, 136)
            for b in range(4):
                lo = d1[rows(40 + n * 136, 136), :] if b == 0 else c1[2 * b - 1, place, :]
                values = jnp.concatenate([lo, c1[2 * b, place, :]], axis=1)
                result = times(values, m1t)
                s1[0, b, place, :] = result[:, :128]
                s1[1, b, place, :] = result[:, 128:]

        loop(5, time_up1)

        def x_up1(k):
            for th in range(2):
                for yb in range(2):
                    e = [s1[th, b, rows((k + d) * 40, 40), :] for d in (1, 0) for b in (yb, 2 + yb)]
                    p1[th, yb, rows(2 * k * 40, 40), :] = even_of(*e)
                    p1[th, yb, rows((2 * k + 1) * 40, 40), :] = odd_of(*e)

        loop(16, x_up1)

        def y_up1(r):
            for th in range(2):
                e = [p1[th, b, pl.ds(r * 40 + d, 32), :] for d in (8, 7) for b in (0, 1)]
                reb[th, pl.ds(r * 64, 32, stride=2), :] = even_of(*e)
                reb[th, pl.ds(r * 64 + 1, 32, stride=2), :] = odd_of(*e)

        loop(32, y_up1)

    iteration(0)
    iteration(1)

    def finish(r):
        for th in range(2):
            out[r, :, th * 128 : (th + 1) * 128] = reb[th, rows(r * 64, 64), :]

    loop(32, finish, unroll=2)


def solution(mesh):
    nx, ny = mesh.shape["gx"], mesh.shape["gy"]
    m1, m1t = time_matrices(256, 256)
    m2, m2t = time_matrices(128, 128)
    m3, m3t = time_matrices(64, 128)

    def v(*shape):
        return pltpu.VMEM(shape, F32)

    scratch = [
        v(2, 34 * 72, 128), v(4, 16 * 72, 128), v(7, 17 * 40, 128), v(22 * 40, 128),
        v(22 * 40, 128), v(2, 10 * 40, 128), v(4, 10 * 24, 128), v(10 * 24, 128),
        v(10 * 24, 128), v(2, 4 * 24, 128), v(4, 6 * 16, 128),
        v(4, 6 * 16, 128), v(2, 10 * 16, 128), v(10 * 24, 128),
        v(4, 10 * 24, 128), v(2, 18 * 24, 128), v(18 * 40, 128),
        v(2, 4, 17 * 40, 128), v(2, 2, 32 * 40, 128), v(2, 32 * 64, 128), v(2, 32 * 8, 128),
    ]
    for shapes in (
        ((2, 128, 128), (2, 64, 128), (2, 16, 128)),
        ((192, 128), (96, 128), (48, 128)),
        ((224, 128), (112, 128), (56, 128)),
        ((192, 128), (96, 128), (128, 128)),
    ):
        scratch += [v(*shape) for shape in shapes] * 2
    scratch += [pltpu.SemaphoreType.DMA((24,)), pltpu.SemaphoreType.DMA((24,))]

    def on_device(counts):
        return pl.pallas_call(
            functools.partial(kernel, nx, ny),
            out_shape=jax.ShapeDtypeStruct(counts.shape, F32),
            in_specs=[pl.BlockSpec(memory_space=pltpu.VMEM)] * 7,
            out_specs=pl.BlockSpec(memory_space=pltpu.VMEM),
            scratch_shapes=scratch,
            compiler_params=pltpu.CompilerParams(
                collective_id=0, has_side_effects=True, vmem_limit_bytes=48 * 1024 * 1024
            ),
        )(counts, m1, m1t, m2, m2t, m3, m3t)

    spec = P(("grp", "gx"), "gy", None)
    return jax.shard_map(on_device, mesh=mesh, in_specs=(spec,), out_specs=spec, check_vma=False)
```

```python
import functools
import math

import jax
import jax.numpy as jnp
import ml_dtypes
import numpy as np
from jax import lax
from jax.experimental import pallas as pl
from jax.experimental.pallas import tpu as pltpu
from jax.sharding import PartitionSpec as P

ROOT_THREE = math.sqrt(3.0)
TAP_SCALE = 4.0 * math.sqrt(2.0)
H = [
    (1.0 + ROOT_THREE) / TAP_SCALE,
    (3.0 + ROOT_THREE) / TAP_SCALE,
    (3.0 - ROOT_THREE) / TAP_SCALE,
    (1.0 - ROOT_THREE) / TAP_SCALE,
]
G = [H[3], -H[2], H[1], -H[0]]
THRESHOLD = 0.1
MESH = pl.DeviceIdType.MESH
F32 = jnp.float32
BF16 = jnp.bfloat16


def split_matrix(matrix):
    high = matrix.astype(ml_dtypes.bfloat16)
    low = (matrix - high.astype(np.float32)).astype(ml_dtypes.bfloat16)
    return np.stack([high, low])


def time_matrices(length, padded):
    matrix = np.zeros((padded, padded), np.float32)
    for k in range(length // 2):
        for j in range(4):
            matrix[(2 * k + j) % length, k] += H[j]
            matrix[(2 * k + j) % length, length // 2 + k] += G[j]
    return split_matrix(matrix), split_matrix(np.ascontiguousarray(matrix.T))


def times(values, matrix_ref):
    high = values.astype(BF16)
    low = (values - high.astype(F32)).astype(BF16)
    first, second = matrix_ref()
    dot = functools.partial(jnp.dot, preferred_element_type=F32)
    return dot(high, first) + (dot(low, first) + dot(high, second))


def shrink(values):
    return values - jnp.clip(values, -THRESHOLD, THRESHOLD)


def low_of(e):
    return (H[0] * e[0] + H[1] * e[1]) + (H[2] * e[2] + H[3] * e[3])


def high_of(e):
    return (G[0] * e[0] + G[1] * e[1]) + (G[2] * e[2] + G[3] * e[3])


def even_of(lo, hi, lo_before, hi_before):
    return (H[0] * lo + G[0] * hi) + (H[2] * lo_before + G[2] * hi_before)


def odd_of(lo, hi, lo_before, hi_before):
    return (H[1] * lo + G[1] * hi) + (H[3] * lo_before + G[3] * hi_before)


def loop(count, body, unroll=4):
    def step(i, carry):
        body(i)
        return carry

    lax.fori_loop(0, count, step, 0, unroll=unroll)


def rows(start, size):
    return pl.ds(pl.multiple_of(start, 8), size)


def kernel(
    nx, ny,
    counts_hbm, mats_hbm, out, counts, corner_counts, mats,
    t0, a0, c1, e1, t2, a2, c2, e2, t3, a3, c3,
    s3, p3, d2, s2, p2, d1, s1, p1, reb, edge, halo,
    f0x, f0y, f0c, f0xr, f0yr, f0cr,
    f1x, f1y, f1c, f1xr, f1yr, f1cr,
    i1x, i1y, i1c, i1xr, i1yr, i1cr,
    i2x, i2y, i2c, i2xr, i2yr, i2cr,
    local_sem, send_sem, recv_sem,
):
    gx = lax.axis_index("gx")
    gy = lax.axis_index("gy")
    x_after, x_before = lax.rem(gx + 1, nx), lax.rem(gx + nx - 1, nx)
    y_after, y_before = lax.rem(gy + 1, ny), lax.rem(gy + ny - 1, ny)
    before = [{"gx": x_before}, {"gy": y_before}, {"gx": x_before, "gy": y_before}]
    after = [{"gx": x_after}, {"gy": y_after}, {"gx": x_after, "gy": y_after}]

    loads = [
        pltpu.make_async_copy(source, target, local_sem.at[n])
        for n, (source, target) in enumerate(
            [
                (counts_hbm.at[:, 0:8, :], corner_counts),
                (counts_hbm.at[0:2], counts.at[0:2]),
                (mats_hbm, mats),
                (counts_hbm.at[2:32], counts.at[2:32]),
            ]
        )
    ]
    for load in loads:
        load.start()

    def matrix(first_row, size, first_column, width):
        return [
            mats[n, first_row : first_row + size, first_column : first_column + width]
            for n in range(2)
        ]

    barrier = pltpu.get_barrier_semaphore()
    for other in before + after:
        pl.semaphore_signal(barrier, inc=1, device_id=other, device_id_type=MESH)

    def send(round_no, sources, targets, others):
        copies = []
        for n in range(3):
            copy = pltpu.make_async_remote_copy(
                src_ref=sources[n],
                dst_ref=targets[n],
                send_sem=send_sem.at[3 * round_no + n],
                recv_sem=recv_sem.at[3 * round_no + n],
                device_id=others[n],
                device_id_type=MESH,
            )
            copy.start()
            copies.append(copy)
        return copies

    def wait(copies):
        for copy in copies:
            copy.wait()

    def residual(count, rebuilt):
        observed = count.astype(F32) * (1.0 / 64.0)
        weight = 1.0 / (1.0 + jnp.abs(observed))
        if rebuilt is None:
            return weight * observed
        return weight * (observed - rebuilt)

    def iteration(number):
        first = number == 0

        def old(ref, *index):
            return 0.0 if first else ref[index]

        m1 = functools.partial(matrix, 0, 256, 0, 256)
        m1t = functools.partial(matrix, 256, 256, 0, 256)
        m2 = functools.partial(matrix, 512, 128, 0, 128)
        m2t = functools.partial(matrix, 512, 128, 128, 128)
        m3 = functools.partial(matrix, 640, 128, 0, 128)
        m3t = functools.partial(matrix, 640, 128, 128, 128)

        if first:
            loads[0].wait()
            loads[1].wait()
        for i in range(2):
            for th in range(2):
                f0x[th, i * 64 : (i + 1) * 64, :] = residual(
                    counts[i, :, th * 128 : (th + 1) * 128],
                    None if first else reb[th, i * 64 : (i + 1) * 64, :],
                )

        def edge_row(x):
            for th in range(2):
                edge[th, rows(x * 8, 8), :] = residual(
                    corner_counts[x, :, th * 128 : (th + 1) * 128],
                    None if first else reb[th, rows(x * 64, 8), :],
                )

        loop(32, edge_row, unroll=4)
        for th in range(2):
            for j in range(2):
                f0y[th, j * 32 : (j + 1) * 32, :] = edge[th, pl.ds(j, 32, stride=8), :]
            for i in range(2):
                n = th * 8 + i * 4
                f0c[n : n + 4, :] = f0x[th, i * 64 : i * 64 + 4, :]
        if first:
            pl.semaphore_wait(barrier, 6)
        f0 = send(4 * number, [f0x, f0y, f0c], [f0xr, f0yr, f0cr], before)

        if first:
            loads[2].wait()
            loads[3].wait()

        def time_rows(n):
            count = counts[pl.ds(n * 4, 4)].reshape(256, 256)
            if first:
                values = residual(count, None)
            else:
                rebuilt = jnp.concatenate(
                    [reb[0, rows(n * 256, 256), :], reb[1, rows(n * 256, 256), :]], axis=1
                )
                values = residual(count, rebuilt)
            result = times(values, m1)
            for i in range(4):
                for tb in range(2):
                    t0[tb, rows((n * 4 + i) * 72, 64), :] = result[
                        i * 64 : (i + 1) * 64, tb * 128 : (tb + 1) * 128
                    ]

        loop(8, time_rows)
        wait(f0)
        result = times(jnp.concatenate([f0xr[0], f0xr[1]], axis=1), m1)
        for i in range(2):
            for tb in range(2):
                t0[tb, (32 + i) * 72 : (32 + i) * 72 + 64, :] = result[
                    i * 64 : (i + 1) * 64, tb * 128 : (tb + 1) * 128
                ]
        result = times(jnp.concatenate([f0yr[0], f0yr[1]], axis=1), m1)
        for j in range(2):
            for tb in range(2):
                t0[tb, pl.ds(64 + j, 32, stride=72), :] = result[
                    j * 32 : (j + 1) * 32, tb * 128 : (tb + 1) * 128
                ]
        result = times(jnp.concatenate([f0cr[0:8], f0cr[8:16]], axis=1), m1)
        for i in range(2):
            for tb in range(2):
                t0[tb, (32 + i) * 72 + 64 : (32 + i) * 72 + 66, :] = result[
                    i * 4 : i * 4 + 2, tb * 128 : (tb + 1) * 128
                ]

        def x_level1(k):
            for tb in range(2):
                e = [t0[tb, rows((2 * k + j) * 72, 72), :] for j in range(4)]
                a0[tb, rows(k * 72, 72), :] = low_of(e)
                a0[2 + tb, rows(k * 72, 72), :] = high_of(e)

        loop(16, x_level1)

        def y_level1(k):
            for xb in range(2):
                for tb in range(2):
                    e = [a0[2 * xb + tb, pl.ds(k * 72 + j, 32, stride=2), :] for j in range(4)]
                    for yb in range(2):
                        value = high_of(e) if yb else low_of(e)
                        band = 4 * xb + 2 * yb + tb
                        if band == 0:
                            e1[rows(k * 40, 32), :] = value
                        else:
                            place = rows((k + 1) * 40 + 8, 32)
                            c1[band - 1, place, :] = shrink(old(c1, band - 1, place, slice(None)) + value)

        loop(16, y_level1)

        for i in range(6):
            f1x[i * 32 : (i + 1) * 32, :] = e1[i * 40 : i * 40 + 32, :]
            f1c[i * 8 : (i + 1) * 8, :] = e1[i * 40 : i * 40 + 8, :]
            f1y[i * 16 : (i + 1) * 16, :] = e1[pl.ds(i, 16, stride=40), :]
        f1 = send(4 * number + 1, [f1x, f1y, f1c], [f1xr, f1yr, f1cr], before)
        for b in range(7):
            i1x[b * 32 : (b + 1) * 32, :] = c1[b, 16 * 40 + 8 : 17 * 40, :]
            i1y[b * 16 : (b + 1) * 16, :] = c1[b, pl.ds(40 + 39, 16, stride=40), :]
            i1c[b : b + 1, :] = c1[b, 17 * 40 - 1 : 17 * 40, :]
        i1c[7:8, :] = i1c[6:7, :]
        i1 = send(4 * number + 2, [i1x, i1y, i1c], [i1xr, i1yr, i1cr], after)

        def time_up1_own(n):
            place = rows(40 + n * 128, 128)
            for b in range(1, 4):
                values = jnp.concatenate([c1[2 * b - 1, place, :], c1[2 * b, place, :]], axis=1)
                result = times(values, m1t)
                s1[0, b, place, :] = result[:, :128]
                s1[1, b, place, :] = result[:, 128:]

        loop(5, time_up1_own)
        wait(f1)
        for i in range(6):
            e1[(16 + i) * 40 : (16 + i) * 40 + 32, :] = f1xr[i * 32 : (i + 1) * 32, :]
            e1[(16 + i) * 40 + 32 : (17 + i) * 40, :] = f1cr[i * 8 : (i + 1) * 8, :]
            e1[pl.ds(32 + i, 16, stride=40), :] = f1yr[i * 16 : (i + 1) * 16, :]

        def time_level2(n):
            t2[rows(n * 176, 176), :] = times(e1[rows(n * 176, 176), :], m2)

        loop(5, time_level2)

        def x_level2(k):
            e = [t2[rows((2 * k + j) * 40, 40), :] for j in range(4)]
            a2[0, rows(k * 40, 40), :] = low_of(e)
            a2[1, rows(k * 40, 40), :] = high_of(e)

        loop(10, x_level2)

        def y_level2_low(k):
            e = [a2[0, pl.ds(k * 40 + j, 18, stride=2), :] for j in range(4)]
            e2[rows(k * 24, 18), :] = low_of(e)

        loop(10, y_level2_low)

        def y_level2(k):
            place = rows((k + 2) * 24 + 8, 16)
            for xb in range(2):
                e = [a2[xb, pl.ds(k * 40 + j, 16, stride=2), :] for j in range(4)]
                for yb in range(2):
                    value = high_of(e) if yb else low_of(e)
                    b = 2 * xb + yb
                    c2[b, place, :] = shrink(old(c2, b, place, slice(None)) + value)

        loop(8, y_level2)

        t3[...] = times(e2[...], m3)

        def x_level3(k):
            e = [t3[rows((2 * k + j) * 24, 24), :] for j in range(4)]
            a3[0, rows(k * 24, 24), :] = low_of(e)
            a3[1, rows(k * 24, 24), :] = high_of(e)

        loop(4, x_level3)

        lane = lax.broadcasted_iota(jnp.int32, (8, 128), 1)

        def y_level3(k):
            place = rows((k + 2) * 16 + 8, 8)
            for xb in range(2):
                e = [a3[xb, pl.ds(k * 24 + j, 8, stride=2), :] for j in range(4)]
                for yb in range(2):
                    value = high_of(e) if yb else low_of(e)
                    b = 2 * xb + yb
                    value = old(c3, b, place, slice(None)) + value
                    if b == 0:
                        c3[b, place, :] = jnp.where(lane < 32, value, shrink(value))
                    else:
                        c3[b, place, :] = shrink(value)

        loop(4, y_level3)

        for b in range(4):
            for i in range(2):
                n = 2 * b + i
                i2x[n * 16 : (n + 1) * 16, :] = c2[b, (8 + i) * 24 + 8 : (9 + i) * 24, :]
                i2x[128 + n * 8 : 128 + (n + 1) * 8, :] = c3[b, (4 + i) * 16 + 8 : (5 + i) * 16, :]
                i2y[n * 8 : (n + 1) * 8, :] = c2[b, pl.ds(2 * 24 + 22 + i, 8, stride=24), :]
                i2y[64 + n * 4 : 64 + (n + 1) * 4, :] = c3[b, pl.ds(2 * 16 + 14 + i, 4, stride=16), :]
                i2c[n * 2 : n * 2 + 2, :] = c2[b, (9 + i) * 24 - 2 : (9 + i) * 24, :]
                i2c[16 + n * 2 : 18 + n * 2, :] = c3[b, (5 + i) * 16 - 2 : (5 + i) * 16, :]
        i2 = send(4 * number + 3, [i2x, i2y, i2c], [i2xr, i2yr, i2cr], after)

        wait(i1)
        c1[0, 8:40, :] = i1xr[0:32, :]
        c1[0, pl.ds(40 + 7, 16, stride=40), :] = i1yr[0:16, :]
        c1[0, 7:8, :] = i1cr[0:1, :]
        for b in range(1, 4):
            n = (b - 1) * 56
            for tb in range(2):
                d = 2 * b - 1 + tb
                halo[tb, n : n + 32, :] = i1xr[d * 32 : (d + 1) * 32, :]
                halo[tb, n + 32 : n + 48, :] = i1yr[d * 16 : (d + 1) * 16, :]
                halo[tb, n + 55 : n + 56, :] = i1cr[d : d + 1, :]
        result = times(jnp.concatenate([halo[0], halo[1]], axis=1), m1t)
        for b in range(1, 4):
            n = (b - 1) * 56
            for th in range(2):
                part = result[n : n + 56, th * 128 : (th + 1) * 128]
                s1[th, b, 8:40, :] = part[0:32]
                s1[th, b, pl.ds(40 + 7, 16, stride=40), :] = part[32:48]
                s1[th, b, 0:8, :] = part[48:56]

        def x_up1(yb, k):
            for th in range(2):
                e = [s1[th, b, rows((k + d) * 40, 40), :] for d in (1, 0) for b in (yb, 2 + yb)]
                p1[th, yb, rows(2 * k * 40, 40), :] = even_of(*e)
                p1[th, yb, rows((2 * k + 1) * 40, 40), :] = odd_of(*e)

        x_up1_low = functools.partial(x_up1, 0)
        x_up1_high = functools.partial(x_up1, 1)
        loop(16, x_up1_high)
        wait(i2)
        for b in range(4):
            for i in range(2):
                n = 2 * b + i
                c2[b, i * 24 + 8 : (i + 1) * 24, :] = i2xr[n * 16 : (n + 1) * 16, :]
                c3[b, i * 16 + 8 : (i + 1) * 16, :] = i2xr[128 + n * 8 : 128 + (n + 1) * 8, :]
                c2[b, pl.ds(2 * 24 + 6 + i, 8, stride=24), :] = i2yr[n * 8 : (n + 1) * 8, :]
                c3[b, pl.ds(2 * 16 + 6 + i, 4, stride=16), :] = i2yr[64 + n * 4 : 64 + (n + 1) * 4, :]
                c2[b, i * 24 + 6 : i * 24 + 8, :] = i2cr[n * 2 : n * 2 + 2, :]
                c3[b, i * 16 + 6 : i * 16 + 8, :] = i2cr[16 + n * 2 : 18 + n * 2, :]

        for b in range(4):
            s3[b] = times(c3[b], m3t)

        def x_up3(k):
            for yb in range(2):
                e = [s3[b, rows((k + d) * 16, 16), :] for d in (1, 0) for b in (yb, 2 + yb)]
                p3[yb, rows(2 * k * 16, 16), :] = even_of(*e)
                p3[yb, rows((2 * k + 1) * 16, 16), :] = odd_of(*e)

        loop(5, x_up3)

        def y_up3(r):
            e = [p3[b, pl.ds(r * 16 + d, 9), :] for d in (7, 6) for b in (0, 1)]
            d2[pl.ds(r * 24 + 6, 9, stride=2), :] = even_of(*e)
            d2[pl.ds(r * 24 + 7, 9, stride=2), :] = odd_of(*e)

        loop(10, y_up3)

        lanes = lax.broadcasted_iota(jnp.int32, (240, 128), 1)
        s2[0] = times(jnp.where(lanes < 64, d2[...], c2[0]), m2t)
        for b in range(1, 4):
            s2[b] = times(c2[b], m2t)

        def x_up2(k):
            for yb in range(2):
                e = [s2[b, rows((k + d) * 24, 24), :] for d in (1, 0) for b in (yb, 2 + yb)]
                p2[yb, rows(2 * k * 24, 24), :] = even_of(*e)
                p2[yb, rows((2 * k + 1) * 24, 24), :] = odd_of(*e)

        loop(9, x_up2)

        def y_up2(r):
            e = [p2[b, pl.ds(r * 24 + d, 17), :] for d in (7, 6) for b in (0, 1)]
            d1[pl.ds(r * 40 + 6, 17, stride=2), :] = even_of(*e)
            d1[pl.ds(r * 40 + 7, 17, stride=2), :] = odd_of(*e)

        loop(18, y_up2)

        def time_up1(n):
            place = rows(n * 136, 136)
            lo = d1[rows(40 + n * 136, 136), :]
            result = times(jnp.concatenate([lo, c1[0, place, :]], axis=1), m1t)
            s1[0, 0, place, :] = result[:, :128]
            s1[1, 0, place, :] = result[:, 128:]

        loop(5, time_up1)

        loop(16, x_up1_low)

        def y_up1(r):
            for th in range(2):
                e = [p1[th, b, pl.ds(r * 40 + d, 32), :] for d in (8, 7) for b in (0, 1)]
                reb[th, pl.ds(r * 64, 32, stride=2), :] = even_of(*e)
                reb[th, pl.ds(r * 64 + 1, 32, stride=2), :] = odd_of(*e)

        loop(32, y_up1)

    iteration(0)
    iteration(1)

    def finish(r):
        for th in range(2):
            out[r, :, th * 128 : (th + 1) * 128] = reb[th, rows(r * 64, 64), :]

    loop(32, finish, unroll=2)


def solution(mesh):
    nx, ny = mesh.shape["gx"], mesh.shape["gy"]
    m1, m1t = time_matrices(256, 256)
    m2, m2t = time_matrices(128, 128)
    m3, m3t = time_matrices(64, 128)

    mats = np.concatenate(
        [m1, m1t, np.concatenate([m2, m2t], axis=2), np.concatenate([m3, m3t], axis=2)], axis=1
    )

    def v(*shape):
        return pltpu.VMEM(shape, F32)

    scratch = [
        pltpu.VMEM((32, 64, 256), jnp.int32), pltpu.VMEM((32, 8, 256), jnp.int32),
        pltpu.VMEM(mats.shape, BF16),
        v(2, 34 * 72, 128), v(4, 16 * 72, 128), v(7, 17 * 40, 128), v(22 * 40, 128),
        v(22 * 40, 128), v(2, 10 * 40, 128), v(4, 10 * 24, 128), v(10 * 24, 128),
        v(10 * 24, 128), v(2, 4 * 24, 128), v(4, 6 * 16, 128),
        v(4, 6 * 16, 128), v(2, 10 * 16, 128), v(10 * 24, 128),
        v(4, 10 * 24, 128), v(2, 18 * 24, 128), v(18 * 40, 128),
        v(2, 4, 17 * 40, 128), v(2, 2, 32 * 40, 128), v(2, 32 * 64, 128), v(2, 32 * 8, 128),
        v(2, 168, 128),
    ]
    for shapes in (
        ((2, 128, 128), (2, 64, 128), (16, 128)),
        ((192, 128), (96, 128), (48, 128)),
        ((224, 128), (112, 128), (8, 128)),
        ((192, 128), (96, 128), (32, 128)),
    ):
        scratch += [v(*shape) for shape in shapes] * 2
    scratch += [pltpu.SemaphoreType.DMA((4,)), pltpu.SemaphoreType.DMA((24,)), pltpu.SemaphoreType.DMA((24,))]

    def on_device(counts):
        return pl.pallas_call(
            functools.partial(kernel, nx, ny),
            out_shape=jax.ShapeDtypeStruct(counts.shape, F32),
            in_specs=[pl.BlockSpec(memory_space=pltpu.HBM)] * 2,
            out_specs=pl.BlockSpec(memory_space=pltpu.VMEM),
            scratch_shapes=scratch,
            compiler_params=pltpu.CompilerParams(
                collective_id=0, has_side_effects=True, vmem_limit_bytes=60 * 1024 * 1024
            ),
        )(counts, mats)

    spec = P(("grp", "gx"), "gy", None)
    return jax.shard_map(on_device, mesh=mesh, in_specs=(spec,), out_specs=spec, check_vma=False)
```

```python
import functools
import math

import jax
import jax.numpy as jnp
import ml_dtypes
import numpy as np
from jax import lax
from jax.experimental import pallas as pl
from jax.experimental.pallas import tpu as pltpu
from jax.sharding import PartitionSpec as P

ROOT_THREE = math.sqrt(3.0)
TAP_SCALE = 4.0 * math.sqrt(2.0)
H = [
    (1.0 + ROOT_THREE) / TAP_SCALE,
    (3.0 + ROOT_THREE) / TAP_SCALE,
    (3.0 - ROOT_THREE) / TAP_SCALE,
    (1.0 - ROOT_THREE) / TAP_SCALE,
]
G = [H[3], -H[2], H[1], -H[0]]
THRESHOLD = 0.1
MESH = pl.DeviceIdType.MESH
F32 = jnp.float32
BF16 = jnp.bfloat16


def split_matrix(matrix):
    high = matrix.astype(ml_dtypes.bfloat16)
    low = (matrix - high.astype(np.float32)).astype(ml_dtypes.bfloat16)
    return np.stack([high, low])


def time_matrices(length, padded):
    matrix = np.zeros((padded, padded), np.float32)
    for k in range(length // 2):
        for j in range(4):
            matrix[(2 * k + j) % length, k] += H[j]
            matrix[(2 * k + j) % length, length // 2 + k] += G[j]
    return split_matrix(matrix), split_matrix(np.ascontiguousarray(matrix.T))


def times(values, matrix_ref):
    high = values.astype(BF16)
    low = (values - high.astype(F32)).astype(BF16)
    first, second = matrix_ref()
    dot = functools.partial(jnp.dot, preferred_element_type=F32)
    return dot(high, first) + (dot(low, first) + dot(high, second))


def shrink(values):
    return values - jnp.clip(values, -THRESHOLD, THRESHOLD)


def low_of(e):
    return (H[0] * e[0] + H[1] * e[1]) + (H[2] * e[2] + H[3] * e[3])


def high_of(e):
    return (G[0] * e[0] + G[1] * e[1]) + (G[2] * e[2] + G[3] * e[3])


def even_of(lo, hi, lo_before, hi_before):
    return (H[0] * lo + G[0] * hi) + (H[2] * lo_before + G[2] * hi_before)


def odd_of(lo, hi, lo_before, hi_before):
    return (H[1] * lo + G[1] * hi) + (H[3] * lo_before + G[3] * hi_before)


def loop(count, body, unroll=4):
    def step(i, carry):
        body(i)
        return carry

    lax.fori_loop(0, count, step, 0, unroll=unroll)


def rows(start, size):
    return pl.ds(pl.multiple_of(start, 8), size)


def kernel(
    nx, ny,
    counts_hbm, mats_hbm, out, counts, corner_counts, mats,
    t0, a0, c1, e1, t2, a2, c2, e2, t3, a3, c3,
    s3, p3, d2, s2, p2, d1, s1, p1, reb, edge, halo,
    f0x, f0y, f0c, f0xr, f0yr, f0cr,
    f1x, f1y, f1c, f1xr, f1yr, f1cr,
    i1x, i1y, i1c, i1xr, i1yr, i1cr,
    i2x, i2y, i2c, i2xr, i2yr, i2cr,
    local_sem, send_sem, recv_sem,
):
    gx = lax.axis_index("gx")
    gy = lax.axis_index("gy")
    x_after, x_before = lax.rem(gx + 1, nx), lax.rem(gx + nx - 1, nx)
    y_after, y_before = lax.rem(gy + 1, ny), lax.rem(gy + ny - 1, ny)
    before = [{"gx": x_before}, {"gy": y_before}, {"gx": x_before, "gy": y_before}]
    after = [{"gx": x_after}, {"gy": y_after}, {"gx": x_after, "gy": y_after}]

    loads = [
        pltpu.make_async_copy(source, target, local_sem.at[n])
        for n, (source, target) in enumerate(
            [
                (counts_hbm.at[:, 0:8, :], corner_counts),
                (counts_hbm.at[0:2], counts.at[0:2]),
                (mats_hbm, mats),
                (counts_hbm.at[2:32], counts.at[2:32]),
            ]
        )
    ]
    for load in loads:
        load.start()

    def matrix(first_row, size, first_column, width):
        return [
            mats[n, first_row : first_row + size, first_column : first_column + width]
            for n in range(2)
        ]

    barrier = pltpu.get_barrier_semaphore()
    for other in before + after:
        pl.semaphore_signal(barrier, inc=1, device_id=other, device_id_type=MESH)

    def send(round_no, sources, targets, others):
        copies = []
        for n in range(3):
            copy = pltpu.make_async_remote_copy(
                src_ref=sources[n],
                dst_ref=targets[n],
                send_sem=send_sem.at[3 * round_no + n],
                recv_sem=recv_sem.at[3 * round_no + n],
                device_id=others[n],
                device_id_type=MESH,
            )
            copy.start()
            copies.append(copy)
        return copies

    def wait(copies):
        for copy in copies:
            copy.wait()

    def residual(count, rebuilt):
        observed = count.astype(F32) * (1.0 / 64.0)
        weight = 1.0 / (1.0 + jnp.abs(observed))
        if rebuilt is None:
            return weight * observed
        return weight * (observed - rebuilt)

    def iteration(number):
        first = number == 0

        def old(ref, *index):
            return 0.0 if first else ref[index]

        m1 = functools.partial(matrix, 0, 256, 0, 256)
        m1t = functools.partial(matrix, 256, 256, 0, 256)
        m2 = functools.partial(matrix, 512, 128, 0, 128)
        m2t = functools.partial(matrix, 512, 128, 128, 128)
        m3 = functools.partial(matrix, 640, 128, 0, 128)
        m3t = functools.partial(matrix, 640, 128, 128, 128)

        if first:
            loads[0].wait()
            loads[1].wait()
        for i in range(2):
            for th in range(2):
                f0x[th, i * 64 : (i + 1) * 64, :] = residual(
                    counts[i, :, th * 128 : (th + 1) * 128],
                    None if first else reb[th, i * 64 : (i + 1) * 64, :],
                )

        def edge_row(x):
            for th in range(2):
                edge[th, rows(x * 8, 8), :] = residual(
                    corner_counts[x, :, th * 128 : (th + 1) * 128],
                    None if first else reb[th, rows(x * 64, 8), :],
                )

        loop(32, edge_row, unroll=4)
        for th in range(2):
            for j in range(2):
                f0y[th, j * 32 : (j + 1) * 32, :] = edge[th, pl.ds(j, 32, stride=8), :]
            for i in range(2):
                n = th * 8 + i * 4
                f0c[n : n + 4, :] = f0x[th, i * 64 : i * 64 + 4, :]
        if first:
            pl.semaphore_wait(barrier, 6)
        f0 = send(4 * number, [f0x, f0y, f0c], [f0xr, f0yr, f0cr], before)

        if first:
            loads[2].wait()
            loads[3].wait()

        def time_rows(n):
            count = counts[pl.ds(n * 4, 4)].reshape(256, 256)
            if first:
                values = residual(count, None)
            else:
                rebuilt = jnp.concatenate(
                    [reb[0, rows(n * 256, 256), :], reb[1, rows(n * 256, 256), :]], axis=1
                )
                values = residual(count, rebuilt)
            result = times(values, m1)
            for i in range(4):
                for tb in range(2):
                    t0[tb, rows((n * 4 + i) * 72, 64), :] = result[
                        i * 64 : (i + 1) * 64, tb * 128 : (tb + 1) * 128
                    ]

        loop(8, time_rows)
        wait(f0)
        result = times(jnp.concatenate([f0xr[0], f0xr[1]], axis=1), m1)
        for i in range(2):
            for tb in range(2):
                t0[tb, (32 + i) * 72 : (32 + i) * 72 + 64, :] = result[
                    i * 64 : (i + 1) * 64, tb * 128 : (tb + 1) * 128
                ]
        result = times(jnp.concatenate([f0yr[0], f0yr[1]], axis=1), m1)
        for j in range(2):
            for tb in range(2):
                t0[tb, pl.ds(64 + j, 32, stride=72), :] = result[
                    j * 32 : (j + 1) * 32, tb * 128 : (tb + 1) * 128
                ]
        result = times(jnp.concatenate([f0cr[0:8], f0cr[8:16]], axis=1), m1)
        for i in range(2):
            for tb in range(2):
                t0[tb, (32 + i) * 72 + 64 : (32 + i) * 72 + 66, :] = result[
                    i * 4 : i * 4 + 2, tb * 128 : (tb + 1) * 128
                ]

        def x_level1(k):
            for tb in range(2):
                e = [t0[tb, rows((2 * k + j) * 72, 72), :] for j in range(4)]
                a0[tb, rows(k * 72, 72), :] = low_of(e)
                a0[2 + tb, rows(k * 72, 72), :] = high_of(e)

        loop(16, x_level1)

        def y_level1(k):
            for xb in range(2):
                for tb in range(2):
                    e = [a0[2 * xb + tb, pl.ds(k * 72 + j, 32, stride=2), :] for j in range(4)]
                    for yb in range(2):
                        value = high_of(e) if yb else low_of(e)
                        band = 4 * xb + 2 * yb + tb
                        if band == 0:
                            e1[rows(k * 40, 32), :] = value
                        else:
                            place = rows((k + 1) * 40 + 8, 32)
                            c1[band - 1, place, :] = shrink(old(c1, band - 1, place, slice(None)) + value)

        loop(16, y_level1)

        for i in range(6):
            f1x[i * 32 : (i + 1) * 32, :] = e1[i * 40 : i * 40 + 32, :]
            f1c[i * 8 : (i + 1) * 8, :] = e1[i * 40 : i * 40 + 8, :]
            f1y[i * 16 : (i + 1) * 16, :] = e1[pl.ds(i, 16, stride=40), :]
        f1 = send(4 * number + 1, [f1x, f1y, f1c], [f1xr, f1yr, f1cr], before)
        for b in range(7):
            i1x[b * 32 : (b + 1) * 32, :] = c1[b, 16 * 40 + 8 : 17 * 40, :]
            i1y[b * 16 : (b + 1) * 16, :] = c1[b, pl.ds(40 + 39, 16, stride=40), :]
            i1c[b : b + 1, :] = c1[b, 17 * 40 - 1 : 17 * 40, :]
        i1c[7:8, :] = i1c[6:7, :]
        i1 = send(4 * number + 2, [i1x, i1y, i1c], [i1xr, i1yr, i1cr], after)

        def time_up1_own(n):
            place = rows(40 + n * 128, 128)
            for b in range(1, 4):
                values = jnp.concatenate([c1[2 * b - 1, place, :], c1[2 * b, place, :]], axis=1)
                result = times(values, m1t)
                s1[0, b, place, :] = result[:, :128]
                s1[1, b, place, :] = result[:, 128:]

        loop(5, time_up1_own)
        wait(f1)
        for i in range(6):
            e1[(16 + i) * 40 : (16 + i) * 40 + 32, :] = f1xr[i * 32 : (i + 1) * 32, :]
            e1[(16 + i) * 40 + 32 : (17 + i) * 40, :] = f1cr[i * 8 : (i + 1) * 8, :]
            e1[pl.ds(32 + i, 16, stride=40), :] = f1yr[i * 16 : (i + 1) * 16, :]

        def time_level2(n):
            t2[rows(n * 176, 176), :] = times(e1[rows(n * 176, 176), :], m2)

        loop(5, time_level2)

        def x_level2(k):
            e = [t2[rows((2 * k + j) * 40, 40), :] for j in range(4)]
            a2[0, rows(k * 40, 40), :] = low_of(e)
            a2[1, rows(k * 40, 40), :] = high_of(e)

        loop(10, x_level2)

        def y_level2_low(k):
            e = [a2[0, pl.ds(k * 40 + j, 18, stride=2), :] for j in range(4)]
            e2[rows(k * 24, 18), :] = low_of(e)

        loop(10, y_level2_low)

        def y_level2(k):
            place = rows((k + 2) * 24 + 8, 16)
            for xb in range(2):
                e = [a2[xb, pl.ds(k * 40 + j, 16, stride=2), :] for j in range(4)]
                for yb in range(2):
                    value = high_of(e) if yb else low_of(e)
                    b = 2 * xb + yb
                    c2[b, place, :] = shrink(old(c2, b, place, slice(None)) + value)

        loop(8, y_level2)

        t3[...] = times(e2[...], m3)

        def x_level3(k):
            e = [t3[rows((2 * k + j) * 24, 24), :] for j in range(4)]
            a3[0, rows(k * 24, 24), :] = low_of(e)
            a3[1, rows(k * 24, 24), :] = high_of(e)

        loop(4, x_level3)

        lane = lax.broadcasted_iota(jnp.int32, (8, 128), 1)

        def y_level3(k):
            place = rows((k + 2) * 16 + 8, 8)
            for xb in range(2):
                e = [a3[xb, pl.ds(k * 24 + j, 8, stride=2), :] for j in range(4)]
                for yb in range(2):
                    value = high_of(e) if yb else low_of(e)
                    b = 2 * xb + yb
                    value = old(c3, b, place, slice(None)) + value
                    if b == 0:
                        c3[b, place, :] = jnp.where(lane < 32, value, shrink(value))
                    else:
                        c3[b, place, :] = shrink(value)

        loop(4, y_level3)

        for b in range(4):
            for i in range(2):
                n = 2 * b + i
                i2x[n * 16 : (n + 1) * 16, :] = c2[b, (8 + i) * 24 + 8 : (9 + i) * 24, :]
                i2x[128 + n * 8 : 128 + (n + 1) * 8, :] = c3[b, (4 + i) * 16 + 8 : (5 + i) * 16, :]
                i2y[n * 8 : (n + 1) * 8, :] = c2[b, pl.ds(2 * 24 + 22 + i, 8, stride=24), :]
                i2y[64 + n * 4 : 64 + (n + 1) * 4, :] = c3[b, pl.ds(2 * 16 + 14 + i, 4, stride=16), :]
                i2c[n * 2 : n * 2 + 2, :] = c2[b, (9 + i) * 24 - 2 : (9 + i) * 24, :]
                i2c[16 + n * 2 : 18 + n * 2, :] = c3[b, (5 + i) * 16 - 2 : (5 + i) * 16, :]
        i2 = send(4 * number + 3, [i2x, i2y, i2c], [i2xr, i2yr, i2cr], after)

        wait(i1)
        c1[0, 8:40, :] = i1xr[0:32, :]
        c1[0, pl.ds(40 + 7, 16, stride=40), :] = i1yr[0:16, :]
        c1[0, 7:8, :] = i1cr[0:1, :]
        for b in range(1, 4):
            n = (b - 1) * 56
            for tb in range(2):
                d = 2 * b - 1 + tb
                halo[tb, n : n + 32, :] = i1xr[d * 32 : (d + 1) * 32, :]
                halo[tb, n + 32 : n + 48, :] = i1yr[d * 16 : (d + 1) * 16, :]
                halo[tb, n + 55 : n + 56, :] = i1cr[d : d + 1, :]
        result = times(jnp.concatenate([halo[0], halo[1]], axis=1), m1t)
        for b in range(1, 4):
            n = (b - 1) * 56
            for th in range(2):
                part = result[n : n + 56, th * 128 : (th + 1) * 128]
                s1[th, b, 8:40, :] = part[0:32]
                s1[th, b, pl.ds(40 + 7, 16, stride=40), :] = part[32:48]
                s1[th, b, 0:8, :] = part[48:56]

        def x_up1(yb, k):
            for th in range(2):
                e = [s1[th, b, rows((k + d) * 40, 40), :] for d in (1, 0) for b in (yb, 2 + yb)]
                p1[th, yb, rows(2 * k * 40, 40), :] = even_of(*e)
                p1[th, yb, rows((2 * k + 1) * 40, 40), :] = odd_of(*e)

        x_up1_low = functools.partial(x_up1, 0)
        x_up1_high = functools.partial(x_up1, 1)
        loop(16, x_up1_high)
        wait(i2)
        for b in range(4):
            for i in range(2):
                n = 2 * b + i
                c2[b, i * 24 + 8 : (i + 1) * 24, :] = i2xr[n * 16 : (n + 1) * 16, :]
                c3[b, i * 16 + 8 : (i + 1) * 16, :] = i2xr[128 + n * 8 : 128 + (n + 1) * 8, :]
                c2[b, pl.ds(2 * 24 + 6 + i, 8, stride=24), :] = i2yr[n * 8 : (n + 1) * 8, :]
                c3[b, pl.ds(2 * 16 + 6 + i, 4, stride=16), :] = i2yr[64 + n * 4 : 64 + (n + 1) * 4, :]
                c2[b, i * 24 + 6 : i * 24 + 8, :] = i2cr[n * 2 : n * 2 + 2, :]
                c3[b, i * 16 + 6 : i * 16 + 8, :] = i2cr[16 + n * 2 : 18 + n * 2, :]

        for b in range(4):
            s3[b] = times(c3[b], m3t)

        def x_up3(k):
            for yb in range(2):
                e = [s3[b, rows((k + d) * 16, 16), :] for d in (1, 0) for b in (yb, 2 + yb)]
                p3[yb, rows(2 * k * 16, 16), :] = even_of(*e)
                p3[yb, rows((2 * k + 1) * 16, 16), :] = odd_of(*e)

        loop(5, x_up3)

        def y_up3(r):
            e = [p3[b, pl.ds(r * 16 + d, 9), :] for d in (7, 6) for b in (0, 1)]
            d2[pl.ds(r * 24 + 6, 9, stride=2), :] = even_of(*e)
            d2[pl.ds(r * 24 + 7, 9, stride=2), :] = odd_of(*e)

        loop(10, y_up3)

        lanes = lax.broadcasted_iota(jnp.int32, (240, 128), 1)
        s2[0] = times(jnp.where(lanes < 64, d2[...], c2[0]), m2t)
        for b in range(1, 4):
            s2[b] = times(c2[b], m2t)

        def x_up2(k):
            for yb in range(2):
                e = [s2[b, rows((k + d) * 24, 24), :] for d in (1, 0) for b in (yb, 2 + yb)]
                p2[yb, rows(2 * k * 24, 24), :] = even_of(*e)
                p2[yb, rows((2 * k + 1) * 24, 24), :] = odd_of(*e)

        loop(9, x_up2)

        def y_up2(r):
            e = [p2[b, pl.ds(r * 24 + d, 17), :] for d in (7, 6) for b in (0, 1)]
            d1[pl.ds(r * 40 + 6, 17, stride=2), :] = even_of(*e)
            d1[pl.ds(r * 40 + 7, 17, stride=2), :] = odd_of(*e)

        loop(18, y_up2)

        def time_up1(n):
            place = rows(n * 136, 136)
            lo = d1[rows(40 + n * 136, 136), :]
            result = times(jnp.concatenate([lo, c1[0, place, :]], axis=1), m1t)
            s1[0, 0, place, :] = result[:, :128]
            s1[1, 0, place, :] = result[:, 128:]

        loop(5, time_up1)

        loop(16, x_up1_low)

        def y_up1(r):
            for th in range(2):
                e = [p1[th, b, pl.ds(r * 40 + d, 32), :] for d in (8, 7) for b in (0, 1)]
                reb[th, pl.ds(r * 64, 32, stride=2), :] = even_of(*e)
                reb[th, pl.ds(r * 64 + 1, 32, stride=2), :] = odd_of(*e)

        loop(32, y_up1)

    iteration(0)
    iteration(1)

    def finish(r):
        for th in range(2):
            out[r, :, th * 128 : (th + 1) * 128] = reb[th, rows(r * 64, 64), :]

    loop(32, finish, unroll=2)


def solution(mesh):
    nx, ny = mesh.shape["gx"], mesh.shape["gy"]
    m1, m1t = time_matrices(256, 256)
    m2, m2t = time_matrices(128, 128)
    m3, m3t = time_matrices(64, 128)

    mats = np.concatenate(
        [m1, m1t, np.concatenate([m2, m2t], axis=2), np.concatenate([m3, m3t], axis=2)], axis=1
    )

    def v(*shape):
        return pltpu.VMEM(shape, F32)

    scratch = [
        pltpu.VMEM((32, 64, 256), jnp.int32), pltpu.VMEM((32, 8, 256), jnp.int32),
        pltpu.VMEM(mats.shape, BF16),
        v(2, 34 * 72, 128), v(4, 16 * 72, 128), v(7, 17 * 40, 128), v(22 * 40, 128),
        v(22 * 40, 128), v(2, 10 * 40, 128), v(4, 10 * 24, 128), v(10 * 24, 128),
        v(10 * 24, 128), v(2, 4 * 24, 128), v(4, 6 * 16, 128),
        v(4, 6 * 16, 128), v(2, 10 * 16, 128), v(10 * 24, 128),
        v(4, 10 * 24, 128), v(2, 18 * 24, 128), v(18 * 40, 128),
        v(2, 4, 17 * 40, 128), v(2, 2, 32 * 40, 128), v(2, 32 * 64, 128), v(2, 32 * 8, 128),
        v(2, 168, 128),
    ]
    for shapes in (
        ((2, 128, 128), (2, 64, 128), (16, 128)),
        ((192, 128), (96, 128), (48, 128)),
        ((224, 128), (112, 128), (8, 128)),
        ((192, 128), (96, 128), (32, 128)),
    ):
        scratch += [v(*shape) for shape in shapes] * 2
    scratch += [pltpu.SemaphoreType.DMA((4,)), pltpu.SemaphoreType.DMA((24,)), pltpu.SemaphoreType.DMA((24,))]

    def on_device(counts):
        return pl.pallas_call(
            functools.partial(kernel, nx, ny),
            out_shape=jax.ShapeDtypeStruct(counts.shape, F32),
            in_specs=[pl.BlockSpec(memory_space=pltpu.HBM)] * 2,
            out_specs=pl.BlockSpec(memory_space=pltpu.VMEM),
            scratch_shapes=scratch,
            compiler_params=pltpu.CompilerParams(
                collective_id=0, has_side_effects=True, vmem_limit_bytes=50 * 1024 * 1024
            ),
        )(counts, mats)

    spec = P(("grp", "gx"), "gy", None)
    return jax.shard_map(on_device, mesh=mesh, in_specs=(spec,), out_specs=spec, check_vma=False)
```
